256 devices in a mesh: tgt: 32 (over z, x), src: 8 (over y, core).
Axes of the slice: x: 4, y: 4, z: 8, core: 2. Of those that a mesh axis runs over, the one named last changes fastest.
Arguments:
- sources: bfloat16 [1024, 1024], P('src', 'tgt'), as said below
- targets: bfloat16 [32768, 1024], P('tgt'), as said below
- fwd_idx: int32 [1024, 16], P('src'), may hold values from 0 to 32767
- bwd_idx: int32 [32768, 16], P('tgt'), may hold values from 0 to 1023
- bwd_len: int32 [32768], P('tgt'), may hold values from 1 to 16
Outputs:
- margin: float32 [1024, 16], P('src')
The draws below stay inside these ranges and needn't reach their ends.
Inputs may be any that keep to these rules, and one draw needn't show every extreme that they name: `sources`: entries are non-negative. `targets`: entries are non-negative.
All inputs are finite; a program needn't handle non-finite values.
Results may differ from the reference program's by a relative error of at most 0.0003.
Values may be sent and summed in bfloat16 or wider, within the bound.
No kernel may reach another device: no remote copies, remote signals or barrier semaphores. Data moves between devices by JAX's collectives and lax.ppermute only.
A program may use at most 64 MiB of HBM per device.

```python
import math
import jax
import jax.numpy as jnp
from jax import lax

D = 1024
K = 16
TGT_DEV = 1024
NT = 32768
NS = 1024
N_TGT = 32


def column_scale(key):
    return jnp.exp(jax.random.uniform(jax.random.fold_in(key, 11), (D,), jnp.float32, math.log(0.3), math.log(3.0)))


def shaped_rows(key, magnitude, density, scales):
    count = magnitude.shape[0]
    keep = jax.random.uniform(jax.random.fold_in(key, 23), (count, D), jnp.float32)
    mask = jnp.where(keep < density[:, None], 1.0, 0.0)
    return (0.05 + mask * magnitude) * scales[None, :]


def draw_sources(key, part):
    scales = column_scale(key)
    key = jax.random.fold_in(key, 1)
    magnitude = jnp.abs(jax.random.normal(jax.random.fold_in(key, 21), (NS, D), jnp.float32))
    density = jax.random.uniform(jax.random.fold_in(key, 22), (NS,), jnp.float32, 0.05, 1.0)
    return shaped_rows(key, magnitude, density, scales).astype(jnp.bfloat16)


def draw_targets(key, part):
    scales = column_scale(key)
    key = jax.random.fold_in(key, 2)
    magnitude = jnp.abs(jax.random.normal(jax.random.fold_in(key, 21), (NT, D), jnp.float32))
    density = jax.random.uniform(jax.random.fold_in(key, 22), (NT,), jnp.float32, 0.05, 1.0)
    return shaped_rows(key, magnitude, density, scales).astype(jnp.bfloat16)


def place_ends(drawn, own_key, low, top_value):
    longest = drawn.shape.index(max(drawn.shape))
    spots = []
    for shift in (0, 1):
        where = [jax.random.randint(jax.random.fold_in(own_key, axis), (), 0, length) for axis, length in enumerate(drawn.shape)]
        where[longest] = (where[longest] + shift) % drawn.shape[longest]
        spots.append(tuple(where))
    return drawn.at[spots[0]].set(low).at[spots[1]].set(top_value)


def setup_inputs(seed: int = 0) -> dict:
    key_list = jax.random.split(jax.random.key(seed), 6)
    sources = draw_sources(jax.random.fold_in(key_list[5], 71), 0)
    targets = draw_targets(jax.random.fold_in(key_list[5], 71), 0)
    fwd_idx = place_ends(jax.random.randint(key_list[2], (NS, K), 0, NT), jax.random.fold_in(key_list[2], 1), 0, NT - 1).astype(jnp.int32)
    bwd_idx = place_ends(jax.random.randint(key_list[3], (NT, K), 0, NS), jax.random.fold_in(key_list[3], 1), 0, NS - 1).astype(jnp.int32)
    bwd_len = place_ends(jax.random.randint(key_list[4], (NT,), 1, K + 1), jax.random.fold_in(key_list[4], 1), 1, K).astype(jnp.int32)
    return dict(sources=sources, targets=targets, fwd_idx=fwd_idx, bwd_idx=bwd_idx, bwd_len=bwd_len)


def reference(sources, targets, fwd_idx, bwd_idx, bwd_len):
    src_full = sources.astype(jnp.float32)
    tgt_full = targets.astype(jnp.float32)
    src_scale = lax.rsqrt(lax.optimization_barrier(jnp.sum(src_full * src_full, axis=1)) + 1e-06)
    tgt_scale = lax.rsqrt(lax.optimization_barrier(jnp.sum(tgt_full * tgt_full, axis=1)) + 1e-06)
    picked_tgt = tgt_full[fwd_idx]
    cand_cos = jnp.einsum('sd,skd->sk', src_full, picked_tgt) * tgt_scale[fwd_idx] * src_scale[:, None]

    def backward_block(packed):
        block_tgt, block_scale, block_idx, block_len = packed
        neighbours = src_full[block_idx]
        sims = jnp.einsum('jd,jkd->jk', block_tgt, neighbours) * block_scale[:, None] * src_scale[block_idx]
        counted = jnp.arange(K)[None, :] < block_len[:, None]
        return lax.optimization_barrier(jnp.sum(jnp.where(counted, sims, 0.0), axis=1)) / block_len.astype(jnp.float32)
    bwd_mean = lax.map(backward_block, (tgt_full.reshape(N_TGT, TGT_DEV, D), tgt_scale.reshape(N_TGT, TGT_DEV), bwd_idx.reshape(N_TGT, TGT_DEV, K), bwd_len.reshape(N_TGT, TGT_DEV))).reshape(NT)
    cand_bwd = bwd_mean[fwd_idx]
    fwd_mean = lax.optimization_barrier(jnp.mean(cand_cos, axis=1))
    return cand_cos / ((fwd_mean[:, None] + cand_bwd) * 0.5)
```

```python
import jax
import jax.numpy as jnp
from jax import lax
from jax.sharding import Mesh, PartitionSpec as P

Z, X, Y, CORE = 8, 4, 4, 2
TGT = ("z", "x")
SRC = ("y", "core")


def spread(block, axes, count):
    copies = jnp.broadcast_to(block[None], (count,) + block.shape)
    return lax.all_to_all(copies, axes, 0, 0)


def body(sources, targets, fwd_idx, bwd_idx, bwd_len):
    tgt_rows, features = targets.shape
    group_rows, neighbours = fwd_idx.shape
    tgt_float = targets.astype(jnp.float32)
    tgt_scale = lax.rsqrt(jnp.sum(tgt_float * tgt_float, axis=1) + 1e-06)
    gathered = spread(sources.T, TGT, Z * X).reshape(features, group_rows)
    src_float = gathered.astype(jnp.float32)
    src_scale = lax.rsqrt(jnp.sum(src_float * src_float, axis=0) + 1e-06)
    products = jnp.dot(targets, gathered, preferred_element_type=jnp.float32)
    scores = products * tgt_scale[:, None] * src_scale[None, :]
    local_src = bwd_idx - lax.axis_index(SRC) * group_rows
    counted = jnp.arange(neighbours)[None, :] < bwd_len[:, None]
    src_column = jnp.arange(group_rows, dtype=jnp.int32)
    slot_src = jnp.where(counted, local_src, -1).T

    def add_backward(total, slot_column):
        match = slot_column[:, None] == src_column[None, :]
        return (total + jnp.sum(jnp.where(match, scores, 0.0), axis=1), None)

    back_term, unused = lax.scan(add_backward, jnp.zeros((tgt_rows,), jnp.float32), slot_src)
    back_total = jnp.sum(spread(back_term, SRC, Y * CORE), axis=0)
    bwd_mean = back_total / bwd_len.astype(jnp.float32)
    local_tgt = (fwd_idx - lax.axis_index(TGT) * tgt_rows).T
    tgt_column = jnp.arange(tgt_rows, dtype=jnp.int32)

    def pick_forward(slot_column):
        match = tgt_column[:, None] == slot_column[None, :]
        cos_part = jnp.sum(jnp.where(match, scores, 0.0), axis=0)
        bwd_part = jnp.sum(jnp.where(match, bwd_mean[:, None], 0.0), axis=0)
        return (cos_part, bwd_part)

    cos_slots, bwd_slots = lax.map(pick_forward, local_tgt)
    picked = jnp.stack([cos_slots, bwd_slots])
    picked = jnp.sum(spread(picked, "x", X), axis=0)
    picked = jnp.sum(spread(picked, "z", Z), axis=0)
    cand_cos, cand_bwd = picked[0], picked[1]
    fwd_mean = jnp.mean(cand_cos, axis=0)
    return (cand_cos / ((fwd_mean[None, :] + cand_bwd) * 0.5)).T


def solution(mesh):
    grid = Mesh(mesh.devices.reshape(Z, X, Y, CORE), TGT + SRC)
    in_specs = (P(SRC, TGT), P(TGT, None), P(SRC, None), P(TGT, None), P(TGT))
    return jax.shard_map(body, mesh=grid, in_specs=in_specs, out_specs=P(SRC, None), check_vma=False)
```

```python
import jax
import jax.numpy as jnp
from jax import lax
from jax.experimental import pallas as pl
from jax.experimental.pallas import tpu as pltpu
from jax.sharding import Mesh, PartitionSpec as P

Z, X, Y, CORE = 8, 4, 4, 2
TGT = ("z", "x")
SRC = ("y", "core")
LANES = 128
VMEM_BYTES = 24 * 1024 * 1024


def take_rows(rows, index):
    return jnp.take_along_axis(rows, index, axis=0)


def take_lanes(rows, index):
    return jnp.take_along_axis(rows, index, axis=1)


def pick_from_tiles(block, index, first_row, picked):
    tile, row = index >> 3, index & 7
    for i in range(block.shape[0] // 8):
        match = tile == (first_row // 8 + i)
        rows = block[8 * i : 8 * i + 8, :]
        picked = [
            jnp.where(match[8 * h : 8 * h + 8], take_rows(rows, row[8 * h : 8 * h + 8]), picked[h])
            for h in range(len(picked))
        ]
    return picked


def pick_from_table(table, index):
    high, low = index >> 7, index & 127
    picked = [jnp.zeros((8, LANES), jnp.float32)] * 2
    for i in range(table.shape[0]):
        row = jnp.broadcast_to(table[i : i + 1, :], (8, LANES))
        picked = [
            jnp.where(high[8 * h : 8 * h + 8] == i, take_lanes(row, low[8 * h : 8 * h + 8]), picked[h])
            for h in range(2)
        ]
    return jnp.concatenate(picked, axis=0)


def score_kernel(place_ref, src_ref, tgt_ref, scale_ref, bwd_ref, len_ref, fwd_ref, out_ref):
    fwd_local = fwd_ref[...] - place_ref[0]
    src = src_ref[...]
    src_float = src.astype(jnp.float32)
    src_scale = lax.rsqrt(jnp.sum(src_float * src_float, axis=0, keepdims=True) + 1e-06)
    tgt_scale = scale_ref[...]
    slot = lax.broadcasted_iota(jnp.int32, (16, LANES), 0)
    cos = [jnp.zeros((8, LANES), jnp.float32)] * 2
    back = []
    for c in range(tgt_ref.shape[0] // LANES):
        lanes = slice(LANES * c, LANES * c + LANES)
        block = jnp.dot(tgt_ref[lanes, :], src, preferred_element_type=jnp.float32) * src_scale
        cos = pick_from_tiles(block, fwd_local, LANES * c, cos)
        bwd_local = bwd_ref[:, lanes] - place_ref[1]
        zero = [jnp.zeros((8, LANES), jnp.float32)] * 2
        sims = jnp.concatenate(pick_from_tiles(block.T, bwd_local, 0, zero), axis=0)
        length = len_ref[c : c + 1, :]
        total = jnp.sum(jnp.where(slot < length, sims, 0.0), axis=0, keepdims=True)
        back.append(total * tgt_scale[c : c + 1, :] / length.astype(jnp.float32))
    cos = jnp.concatenate(cos, axis=0) * pick_from_table(tgt_scale, fwd_local)
    sent = jnp.concatenate(back + [cos], axis=0)
    for d in range(out_ref.shape[0]):
        out_ref[d] = sent


def mean_kernel(place_ref, got_ref, fwd_ref, out_ref):
    groups = got_ref.shape[0] // X
    table, cos = [], jnp.zeros((16, LANES), jnp.float32)
    for x in range(X):
        total = got_ref[x * groups, :8, :]
        for g in range(1, groups):
            total = total + got_ref[x * groups + g, :8, :]
        table.append(total)
        cos = cos + got_ref[x * groups + place_ref[1], 8:, :]
    bwd = pick_from_table(jnp.concatenate(table, axis=0), fwd_ref[...] - place_ref[0])
    for d in range(out_ref.shape[0]):
        out_ref[d, :16, :] = cos
        out_ref[d, 16:, :] = bwd


def margin_kernel(got_ref, out_ref):
    total = jnp.sum(got_ref[...], axis=0)
    cos, bwd = total[:16], total[16:]
    fwd_mean = jnp.mean(cos, axis=0, keepdims=True)
    out_ref[...] = cos / ((fwd_mean + bwd) * 0.5)


def call(kernel, shape, specs, *args):
    return pl.pallas_call(
        kernel,
        out_shape=jax.ShapeDtypeStruct(shape, jnp.float32),
        in_specs=[pl.BlockSpec(memory_space=s) for s in specs],
        out_specs=pl.BlockSpec(memory_space=pltpu.VMEM),
        compiler_params=pltpu.CompilerParams(vmem_limit_bytes=VMEM_BYTES),
    )(*args)


def body(sources, targets, fwd_idx, bwd_idx, bwd_len):
    tgt_rows, features = targets.shape
    group_rows, neighbours = fwd_idx.shape
    smem, vmem = pltpu.SMEM, pltpu.VMEM
    tgt_index = lax.axis_index(TGT)
    src_index = lax.axis_index(SRC)
    fwd = fwd_idx.T
    copies = jnp.broadcast_to(sources.T[None], (Z * X,) + sources.T.shape)
    gathered = lax.all_to_all(copies, TGT, 0, 0).reshape(features, group_rows)
    tgt_float = targets.astype(jnp.float32)
    tgt_scale = lax.rsqrt(jnp.sum(tgt_float * tgt_float, axis=1) + 1e-06)
    place = jnp.stack([tgt_index * tgt_rows, src_index * group_rows]).astype(jnp.int32)
    sent = call(
        score_kernel, (X * Y * CORE, 24, LANES), [smem] + [vmem] * 6,
        place, gathered, targets, tgt_scale.reshape(-1, LANES), bwd_idx.T, bwd_len.reshape(-1, LANES), fwd,
    )
    got = lax.all_to_all(sent, ("x",) + SRC, 0, 0)
    place = jnp.stack([lax.axis_index("z") * (X * tgt_rows), src_index]).astype(jnp.int32)
    sent = call(mean_kernel, (Z, 32, LANES), [smem] + [vmem] * 2, place, got, fwd)
    got = lax.all_to_all(sent, "z", 0, 0)
    return call(margin_kernel, (neighbours, group_rows), [vmem], got).T


def solution(mesh):
    grid = Mesh(mesh.devices.reshape(Z, X, Y, CORE), TGT + SRC)
    in_specs = (P(SRC, TGT), P(TGT, None), P(SRC, None), P(TGT, None), P(TGT))
    return jax.shard_map(body, mesh=grid, in_specs=in_specs, out_specs=P(SRC, None), check_vma=False)
```

```python
import jax
import jax.numpy as jnp
from jax import lax
from jax.experimental import pallas as pl
from jax.experimental.pallas import tpu as pltpu
from jax.sharding import Mesh, PartitionSpec as P

Z, X, Y, CORE = 8, 4, 4, 2
TGT = ("z", "x")
SRC = ("y", "core")
LANES = 128
VMEM_BYTES = 24 * 1024 * 1024


def take_rows(rows, index):
    return jnp.take_along_axis(rows, index, axis=0)


def take_lanes(rows, index):
    return jnp.take_along_axis(rows, index, axis=1)


def pick_from_tiles(block, index, first_row, picked):
    tile, row = index >> 3, index & 7
    for i in range(block.shape[0] // 8):
        match = tile == (first_row // 8 + i)
        rows = block[8 * i : 8 * i + 8, :]
        picked = [
            jnp.where(match[8 * h : 8 * h + 8], take_rows(rows, row[8 * h : 8 * h + 8]), picked[h])
            for h in range(len(picked))
        ]
    return picked


def pick_from_table(table, index):
    high, low = index >> 7, index & 127
    picked = [jnp.zeros((8, LANES), jnp.float32)] * 2
    for i in range(table.shape[0]):
        row = jnp.broadcast_to(table[i : i + 1, :], (8, LANES))
        picked = [
            jnp.where(high[8 * h : 8 * h + 8] == i, take_lanes(row, low[8 * h : 8 * h + 8]), picked[h])
            for h in range(2)
        ]
    return jnp.concatenate(picked, axis=0)


def score_kernel(src_ref, tgt_ref, bwd_ref, len_ref, fwd_ref, out_ref):
    fwd_local = fwd_ref[...] - lax.axis_index(TGT) * tgt_ref.shape[0]
    first_src = lax.axis_index(SRC) * LANES
    src = src_ref[...]
    src_float = src.astype(jnp.float32)
    src_scale = lax.rsqrt(jnp.sum(src_float * src_float, axis=0, keepdims=True) + 1e-06)
    slot = lax.broadcasted_iota(jnp.int32, (16, LANES), 0)
    cos = [jnp.zeros((8, LANES), jnp.float32)] * 2
    back, scales = [], []
    for c in range(tgt_ref.shape[0] // LANES):
        lanes = slice(LANES * c, LANES * c + LANES)
        rows = tgt_ref[lanes, :]
        tgt_float = rows.astype(jnp.float32)
        squares = tgt_float * tgt_float
        part = squares[:, :LANES]
        for f in range(LANES, squares.shape[1], LANES):
            part = part + squares[:, f : f + LANES]
        tgt_scale = lax.rsqrt(jnp.sum(part.T, axis=0, keepdims=True) + 1e-06)
        scales.append(tgt_scale)
        block = jnp.dot(rows, src, preferred_element_type=jnp.float32) * src_scale
        cos = pick_from_tiles(block, fwd_local, LANES * c, cos)
        bwd_local = bwd_ref[:, lanes] - first_src
        zero = [jnp.zeros((8, LANES), jnp.float32)] * 2
        sims = jnp.concatenate(pick_from_tiles(block.T, bwd_local, 0, zero), axis=0)
        length = len_ref[c : c + 1, :]
        total = jnp.sum(jnp.where(slot < length, sims, 0.0), axis=0, keepdims=True)
        back.append(total * tgt_scale / length.astype(jnp.float32))
    cos = jnp.concatenate(cos, axis=0) * pick_from_table(jnp.concatenate(scales, axis=0), fwd_local)
    sent = jnp.concatenate(back + [cos], axis=0)
    for d in range(out_ref.shape[0]):
        out_ref[d] = sent


def mean_kernel(got_ref, fwd_ref, out_ref):
    group = lax.axis_index(SRC)
    first_tgt = lax.axis_index("z") * (X * 8 * LANES)
    groups = got_ref.shape[0] // X
    table, cos = [], jnp.zeros((16, LANES), jnp.float32)
    for x in range(X):
        total = got_ref[x * groups, :8, :]
        for g in range(1, groups):
            total = total + got_ref[x * groups + g, :8, :]
        table.append(total)
        cos = cos + got_ref[x * groups + group, 8:, :]
    bwd = pick_from_table(jnp.concatenate(table, axis=0), fwd_ref[...] - first_tgt)
    for d in range(out_ref.shape[0]):
        out_ref[d, :16, :] = cos
        out_ref[d, 16:, :] = bwd


def margin_kernel(got_ref, out_ref):
    total = jnp.sum(got_ref[...], axis=0)
    cos, bwd = total[:16], total[16:]
    fwd_mean = jnp.mean(cos, axis=0, keepdims=True)
    out_ref[...] = cos / ((fwd_mean + bwd) * 0.5)


def call(kernel, shape, *args):
    return pl.pallas_call(
        kernel,
        out_shape=jax.ShapeDtypeStruct(shape, jnp.float32),
        in_specs=[pl.BlockSpec(memory_space=pltpu.VMEM)] * len(args),
        out_specs=pl.BlockSpec(memory_space=pltpu.VMEM),
        compiler_params=pltpu.CompilerParams(vmem_limit_bytes=VMEM_BYTES),
    )(*args)


def body(sources, targets, fwd_idx, bwd_idx, bwd_len):
    features = targets.shape[1]
    group_rows, neighbours = fwd_idx.shape
    fwd = fwd_idx.T
    copies = jnp.broadcast_to(sources.T[None], (Z * X,) + sources.T.shape)
    gathered = lax.all_to_all(copies, TGT, 0, 0).reshape(features, group_rows)
    sent = call(
        score_kernel, (X * Y * CORE, 24, LANES), gathered, targets, bwd_idx.T, bwd_len.reshape(-1, LANES), fwd
    )
    got = lax.all_to_all(sent, ("x",) + SRC, 0, 0)
    sent = call(mean_kernel, (Z, 32, LANES), got, fwd)
    got = lax.all_to_all(sent, "z", 0, 0)
    return call(margin_kernel, (neighbours, group_rows), got).T


def solution(mesh):
    grid = Mesh(mesh.devices.reshape(Z, X, Y, CORE), TGT + SRC)
    in_specs = (P(SRC, TGT), P(TGT, None), P(SRC, None), P(TGT, None), P(TGT))
    return jax.shard_map(body, mesh=grid, in_specs=in_specs, out_specs=P(SRC, None), check_vma=False)
```

```python
import jax
import jax.numpy as jnp
from jax import lax
from jax.experimental import pallas as pl
from jax.experimental.pallas import tpu as pltpu
from jax.sharding import Mesh, PartitionSpec as P

Z, X, Y, CORE = 8, 4, 4, 2
TGT = ("z", "x")
SRC = ("y", "core")
LANES = 128
VMEM_BYTES = 24 * 1024 * 1024


def take_rows(rows, index):
    return jnp.take_along_axis(rows, index, axis=0)


def take_lanes(rows, index):
    return jnp.take_along_axis(rows, index, axis=1)


def pick_from_tiles(block, index, first_row, picked):
    tile, row = index >> 3, index & 7
    for i in range(block.shape[0] // 8):
        match = tile == (first_row // 8 + i)
        rows = block[8 * i : 8 * i + 8, :]
        picked = [
            jnp.where(match[8 * h : 8 * h + 8], take_rows(rows, row[8 * h : 8 * h + 8]), picked[h])
            for h in range(len(picked))
        ]
    return picked


def pick_from_table(table, index):
    high, low = index >> 7, index & 127
    picked = [jnp.zeros((8, LANES), jnp.float32)] * 2
    for i in range(table.shape[0]):
        row = jnp.broadcast_to(table[i : i + 1, :], (8, LANES))
        picked = [
            jnp.where(high[8 * h : 8 * h + 8] == i, take_lanes(row, low[8 * h : 8 * h + 8]), picked[h])
            for h in range(2)
        ]
    return jnp.concatenate(picked, axis=0)


def score_kernel(src_ref, tgt_hbm, bwd_hbm, len_hbm, fwd_hbm, out_ref, fwd_ref, tgt_ref, bwd_ref, len_ref, sems):
    pairs = ((tgt_hbm, tgt_ref), (bwd_hbm, bwd_ref), (len_hbm, len_ref), (fwd_hbm, fwd_ref))
    loads = [pltpu.make_async_copy(hbm, ref, sems.at[i]) for i, (hbm, ref) in enumerate(pairs)]
    for load in loads:
        load.start()
    src = src_ref[...]
    src_float = src.astype(jnp.float32)
    src_scale = lax.rsqrt(jnp.sum(src_float * src_float, axis=0, keepdims=True) + 1e-06)
    for load in loads:
        load.wait()
    fwd_local = fwd_ref[...] - lax.axis_index(TGT) * tgt_ref.shape[0]
    first_src = lax.axis_index(SRC) * LANES
    slot = lax.broadcasted_iota(jnp.int32, (16, LANES), 0)
    cos = [jnp.zeros((8, LANES), jnp.float32)] * 2
    back, scales = [], []
    for c in range(tgt_ref.shape[0] // LANES):
        lanes = slice(LANES * c, LANES * c + LANES)
        rows = tgt_ref[lanes, :]
        tgt_float = rows.astype(jnp.float32)
        squares = tgt_float * tgt_float
        part = squares[:, :LANES]
        for f in range(LANES, squares.shape[1], LANES):
            part = part + squares[:, f : f + LANES]
        tgt_scale = lax.rsqrt(jnp.sum(part.T, axis=0, keepdims=True) + 1e-06)
        scales.append(tgt_scale)
        block = jnp.dot(rows, src, preferred_element_type=jnp.float32) * src_scale
        cos = pick_from_tiles(block, fwd_local, LANES * c, cos)
        bwd_local = bwd_ref[:, lanes] - first_src
        zero = [jnp.zeros((8, LANES), jnp.float32)] * 2
        sims = jnp.concatenate(pick_from_tiles(block.T, bwd_local, 0, zero), axis=0)
        length = len_ref[c : c + 1, :]
        total = jnp.sum(jnp.where(slot < length, sims, 0.0), axis=0, keepdims=True)
        back.append(total * tgt_scale / length.astype(jnp.float32))
    cos = jnp.concatenate(cos, axis=0) * pick_from_table(jnp.concatenate(scales, axis=0), fwd_local)
    sent = jnp.concatenate(back + [cos], axis=0)
    for d in range(out_ref.shape[0]):
        out_ref[d] = sent


def mean_kernel(got_ref, fwd_ref, out_ref):
    group = lax.axis_index(SRC)
    first_tgt = lax.axis_index("z") * (X * 8 * LANES)
    groups = got_ref.shape[0] // X
    table, cos = [], jnp.zeros((16, LANES), jnp.float32)
    for x in range(X):
        total = got_ref[x * groups, :8, :]
        for g in range(1, groups):
            total = total + got_ref[x * groups + g, :8, :]
        table.append(total)
        cos = cos + got_ref[x * groups + group, 8:, :]
    bwd = pick_from_table(jnp.concatenate(table, axis=0), fwd_ref[...] - first_tgt)
    for d in range(out_ref.shape[0]):
        out_ref[d, :16, :] = cos
        out_ref[d, 16:, :] = bwd


def margin_kernel(got_ref, out_ref):
    total = jnp.sum(got_ref[...], axis=0)
    cos, bwd = total[:16], total[16:]
    fwd_mean = jnp.mean(cos, axis=0, keepdims=True)
    out_ref[...] = cos / ((fwd_mean + bwd) * 0.5)


def call(kernel, shapes, memory, *args, scratch=()):
    return pl.pallas_call(
        kernel,
        out_shape=[jax.ShapeDtypeStruct(shape, dtype) for shape, dtype in shapes],
        in_specs=[pl.BlockSpec(memory_space=space) for space in memory],
        out_specs=[pl.BlockSpec(memory_space=pltpu.VMEM)] * len(shapes),
        scratch_shapes=scratch,
        compiler_params=pltpu.CompilerParams(vmem_limit_bytes=VMEM_BYTES),
    )(*args)


def body(sources, targets, fwd_idx, bwd_idx, bwd_len):
    features = targets.shape[1]
    group_rows, neighbours = fwd_idx.shape
    vmem, hbm = pltpu.VMEM, pltpu.HBM
    copies = jnp.broadcast_to(sources.T[None], (Z * X,) + sources.T.shape)
    gathered = lax.all_to_all(copies, TGT, 0, 0).reshape(features, group_rows)
    inputs = (targets, bwd_idx.T, bwd_len.reshape(-1, LANES), fwd_idx.T)
    inputs = [pltpu.with_memory_space_constraint(a, hbm) for a in inputs]
    sent, fwd = call(
        score_kernel,
        [((X * Y * CORE, 24, LANES), jnp.float32), ((neighbours, group_rows), jnp.int32)],
        [vmem] + [hbm] * 4,
        gathered,
        *inputs,
        scratch=[vmem(a.shape, a.dtype) for a in inputs[:3]] + [pltpu.SemaphoreType.DMA((4,))],
    )
    got = lax.all_to_all(sent, ("x",) + SRC, 0, 0)
    (sent,) = call(mean_kernel, [((Z, 32, LANES), jnp.float32)], [vmem] * 2, got, fwd)
    got = lax.all_to_all(sent, "z", 0, 0)
    return call(margin_kernel, [((neighbours, group_rows), jnp.float32)], [vmem], got)[0].T


def solution(mesh):
    grid = Mesh(mesh.devices.reshape(Z, X, Y, CORE), TGT + SRC)
    in_specs = (P(SRC, TGT), P(TGT, None), P(SRC, None), P(TGT, None), P(TGT))
    return jax.shard_map(body, mesh=grid, in_specs=in_specs, out_specs=P(SRC, None), check_vma=False)
```

```python
import jax
import jax.numpy as jnp
from jax import lax
from jax.experimental import pallas as pl
from jax.experimental.pallas import tpu as pltpu
from jax.sharding import Mesh, PartitionSpec as P

BITS = ("z2", "z1", "z0", "x1", "x0", "y1", "y0", "core")
Z_BITS, X_BITS, Y_BITS = BITS[:3], BITS[3:5], BITS[5:7]
TGT = Z_BITS + X_BITS
SRC = BITS[5:]
Z, X, GROUPS = 8, 4, 8
GATHER = ("x1", "x0", "z2", "z1", "z0")
SUM = ("x1", "x0", "y1", "y0")
SPREAD = ("z0", "z1", "z2")
LANES = 128
VMEM_BYTES = 24 * 1024 * 1024


def slot(order, axes, index):
    at = 0
    for n, axis in enumerate(reversed(axes)):
        bit = index >> n & 1
        at = at + bit * (1 << (len(order) - 1 - order.index(axis)))
    return at


def take_rows(rows, index):
    return jnp.take_along_axis(rows, index, axis=0)


def take_lanes(rows, index):
    return jnp.take_along_axis(rows, index, axis=1)


def pick_from_tiles(block, index, first_row, picked):
    tile, row = index >> 3, index & 7
    for i in range(block.shape[0] // 8):
        match = tile == (first_row // 8 + i)
        rows = block[8 * i : 8 * i + 8, :]
        picked = [
            jnp.where(match[8 * h : 8 * h + 8], take_rows(rows, row[8 * h : 8 * h + 8]), picked[h])
            for h in range(len(picked))
        ]
    return picked


def pick_from_table(table, index):
    high, low = index >> 7, index & 127
    picked = [jnp.zeros((8, LANES), jnp.float32)] * 2
    for i in range(table.shape[0]):
        row = jnp.broadcast_to(table[i : i + 1, :], (8, LANES))
        picked = [
            jnp.where(high[8 * h : 8 * h + 8] == i, take_lanes(row, low[8 * h : 8 * h + 8]), picked[h])
            for h in range(2)
        ]
    return jnp.concatenate(picked, axis=0)


def score_kernel(src_ref, tgt_ref, scale_ref, bwd_ref, len_ref, fwd_ref, out_ref):
    src = jnp.concatenate([src_ref[slot(GATHER, TGT, t)] for t in range(Z * X)], axis=0)
    src_float = src.astype(jnp.float32)
    src_scale = lax.rsqrt(jnp.sum(src_float * src_float, axis=0, keepdims=True) + 1e-06)
    fwd_local = fwd_ref[...] - lax.axis_index(TGT) * tgt_ref.shape[0]
    first_src = lax.axis_index(SRC) * LANES
    neighbour = lax.broadcasted_iota(jnp.int32, (16, LANES), 0)
    cos = [jnp.zeros((8, LANES), jnp.float32)] * 2
    tgt_scale, back = scale_ref[...], []
    for c in range(tgt_ref.shape[0] // LANES):
        lanes = slice(LANES * c, LANES * c + LANES)
        block = jnp.dot(tgt_ref[lanes, :], src, preferred_element_type=jnp.float32) * src_scale
        cos = pick_from_tiles(block, fwd_local, LANES * c, cos)
        zero = [jnp.zeros((8, LANES), jnp.float32)] * 2
        sims = jnp.concatenate(pick_from_tiles(block.T, bwd_ref[:, lanes] - first_src, 0, zero), axis=0)
        length = len_ref[c : c + 1, :]
        total = jnp.sum(jnp.where(neighbour < length, sims, 0.0), axis=0, keepdims=True)
        back.append(total * tgt_scale[c : c + 1, :] / length.astype(jnp.float32))
    cos = jnp.concatenate(cos, axis=0) * pick_from_table(tgt_scale, fwd_local)
    out_ref[...] = jnp.concatenate(back + [cos], axis=0)


def join_kernel(own_ref, other_ref, out_ref):
    total = own_ref[:8, :] + other_ref[...]
    for d in range(out_ref.shape[0]):
        out_ref[d, :8, :] = total
        out_ref[d, 8:, :] = own_ref[8:, :]


def mean_kernel(got_ref, fwd_ref, out_ref):
    group = slot(SUM, Y_BITS, lax.axis_index(Y_BITS))
    first_tgt = lax.axis_index(Z_BITS) * (X * 8 * LANES)
    table, cos = [], jnp.zeros((16, LANES), jnp.float32)
    for x in range(X):
        at = slot(SUM, X_BITS, x)
        total = got_ref[at, :8, :]
        for g in range(1, GROUPS // 2):
            total = total + got_ref[at + slot(SUM, Y_BITS, g), :8, :]
        table.append(total)
        cos = cos + got_ref[at + group, 8:, :]
    bwd = pick_from_table(jnp.concatenate(table, axis=0), fwd_ref[...] - first_tgt)
    for d in range(out_ref.shape[0]):
        out_ref[d, :16, :] = cos
        out_ref[d, 16:, :] = bwd


def margin_kernel(got_ref, out_ref):
    total = jnp.sum(got_ref[...], axis=0)
    cos, bwd = total[:16], total[16:]
    fwd_mean = jnp.mean(cos, axis=0, keepdims=True)
    out_ref[...] = cos / ((fwd_mean + bwd) * 0.5)


def call(kernel, shape, *args):
    return pl.pallas_call(
        kernel,
        out_shape=jax.ShapeDtypeStruct(shape, jnp.float32),
        in_specs=[pl.BlockSpec(memory_space=pltpu.VMEM)] * len(args),
        out_specs=pl.BlockSpec(memory_space=pltpu.VMEM),
        compiler_params=pltpu.CompilerParams(vmem_limit_bytes=VMEM_BYTES),
    )(*args)


def body(sources, targets, fwd_idx, bwd_idx, bwd_len):
    group_rows, neighbours = fwd_idx.shape
    fwd = fwd_idx.T
    copies = jnp.broadcast_to(sources.T[None], (Z * X,) + sources.T.shape)
    gathered = lax.all_to_all(copies, GATHER, 0, 0)
    tgt_float = targets.astype(jnp.float32)
    tgt_scale = lax.rsqrt(jnp.sum(tgt_float * tgt_float, axis=1) + 1e-06).reshape(-1, LANES)
    sent = call(
        score_kernel, (24, LANES),
        gathered, targets, tgt_scale, bwd_idx.T, bwd_len.reshape(-1, LANES), fwd,
    )
    other = lax.ppermute(sent[:8], "core", [(0, 1), (1, 0)])
    sent = call(join_kernel, (X * GROUPS // 2, 24, LANES), sent, other)
    got = lax.all_to_all(sent, SUM, 0, 0)
    sent = call(mean_kernel, (Z, 32, LANES), got, fwd)
    got = lax.all_to_all(sent, SPREAD, 0, 0)
    return call(margin_kernel, (neighbours, group_rows), got).T


def solution(mesh):
    grid = Mesh(mesh.devices.reshape((2,) * len(BITS)), BITS)
    in_specs = (P(SRC, TGT), P(TGT, None), P(SRC, None), P(TGT, None), P(TGT))
    return jax.shard_map(body, mesh=grid, in_specs=in_specs, out_specs=P(SRC, None), check_vma=False)
```

```python
import jax
import jax.numpy as jnp
from jax import lax
from jax.experimental import pallas as pl
from jax.experimental.pallas import tpu as pltpu
from jax.sharding import Mesh, PartitionSpec as P

Z, X, Y, CORE = 8, 4, 4, 2
TGT = ("z", "x")
SRC = ("y", "core")
GATHER = [((z + 4) % Z) * X + (x + 2) % X for x in range(X) for z in range(Z)]
SUM = [((x + 2) % X) * Y + (y + 2) % Y for x in range(X) for y in range(Y)]
SPREAD = [(z + 4) % Z for z in (0, 4, 2, 6, 1, 5, 3, 7)]
LANES = 128
VMEM_BYTES = 24 * 1024 * 1024


def take_rows(rows, index):
    return jnp.take_along_axis(rows, index, axis=0)


def take_lanes(rows, index):
    return jnp.take_along_axis(rows, index, axis=1)


def pick_from_tiles(block, index, first_row, picked):
    tile, row = index >> 3, index & 7
    for i in range(block.shape[0] // 8):
        match = tile == (first_row // 8 + i)
        rows = block[8 * i : 8 * i + 8, :]
        picked = [
            jnp.where(match[8 * h : 8 * h + 8], take_rows(rows, row[8 * h : 8 * h + 8]), picked[h])
            for h in range(len(picked))
        ]
    return picked


def pick_from_table(table, index):
    high, low = index >> 7, index & 127
    picked = [jnp.zeros((8, LANES), jnp.float32)] * 2
    for i in range(table.shape[0]):
        row = jnp.broadcast_to(table[i : i + 1, :], (8, LANES))
        picked = [
            jnp.where(high[8 * h : 8 * h + 8] == i, take_lanes(row, low[8 * h : 8 * h + 8]), picked[h])
            for h in range(2)
        ]
    return jnp.concatenate(picked, axis=0)


def score_kernel(src_ref, tgt_ref, scale_ref, bwd_ref, len_ref, fwd_ref, out_ref):
    src = jnp.concatenate([src_ref[GATHER.index(t)] for t in range(Z * X)], axis=0)
    src_float = src.astype(jnp.float32)
    src_scale = lax.rsqrt(jnp.sum(src_float * src_float, axis=0, keepdims=True) + 1e-06)
    fwd_local = fwd_ref[...] - lax.axis_index(TGT) * tgt_ref.shape[0]
    first_src = lax.axis_index(SRC) * LANES
    neighbour = lax.broadcasted_iota(jnp.int32, (16, LANES), 0)
    cos = [jnp.zeros((8, LANES), jnp.float32)] * 2
    tgt_scale, back = scale_ref[...], []
    for c in range(tgt_ref.shape[0] // LANES):
        lanes = slice(LANES * c, LANES * c + LANES)
        block = jnp.dot(tgt_ref[lanes, :], src, preferred_element_type=jnp.float32) * src_scale
        cos = pick_from_tiles(block, fwd_local, LANES * c, cos)
        zero = [jnp.zeros((8, LANES), jnp.float32)] * 2
        sims = jnp.concatenate(pick_from_tiles(block.T, bwd_ref[:, lanes] - first_src, 0, zero), axis=0)
        length = len_ref[c : c + 1, :]
        total = jnp.sum(jnp.where(neighbour < length, sims, 0.0), axis=0, keepdims=True)
        back.append(total * tgt_scale[c : c + 1, :] / length.astype(jnp.float32))
    cos = jnp.concatenate(cos, axis=0) * pick_from_table(tgt_scale, fwd_local)
    out_ref[...] = jnp.concatenate(back + [cos], axis=0)


def join_kernel(own_ref, other_ref, out_ref):
    total = own_ref[:8, :] + other_ref[...]
    for d in range(out_ref.shape[0]):
        out_ref[d, :8, :] = total
        out_ref[d, 8:, :] = own_ref[8:, :]


def mean_kernel(got_ref, fwd_ref, out_ref):
    y = lax.axis_index("y")
    first_tgt = lax.axis_index("z") * (X * 8 * LANES)
    table, cos = [], jnp.zeros((16, LANES), jnp.float32)
    for x in range(X):
        parts = [SUM.index(x * Y + line) for line in range(Y)]
        total = got_ref[parts[0], :8, :]
        for at in parts[1:]:
            total = total + got_ref[at, :8, :]
        table.append(total)
        for line, at in enumerate(parts):
            cos = cos + jnp.where(y == line, got_ref[at, 8:, :], 0.0)
    bwd = pick_from_table(jnp.concatenate(table, axis=0), fwd_ref[...] - first_tgt)
    for d in range(out_ref.shape[0]):
        out_ref[d, :16, :] = cos
        out_ref[d, 16:, :] = bwd


def margin_kernel(got_ref, out_ref):
    total = jnp.sum(got_ref[...], axis=0)
    cos, bwd = total[:16], total[16:]
    fwd_mean = jnp.mean(cos, axis=0, keepdims=True)
    out_ref[...] = cos / ((fwd_mean + bwd) * 0.5)


def call(kernel, shape, *args):
    return pl.pallas_call(
        kernel,
        out_shape=jax.ShapeDtypeStruct(shape, jnp.float32),
        in_specs=[pl.BlockSpec(memory_space=pltpu.VMEM)] * len(args),
        out_specs=pl.BlockSpec(memory_space=pltpu.VMEM),
        compiler_params=pltpu.CompilerParams(vmem_limit_bytes=VMEM_BYTES),
    )(*args)


def exchange(blocks, axes, order):
    return lax.all_to_all(blocks, axes, 0, 0, axis_index_groups=[order])


def body(sources, targets, fwd_idx, bwd_idx, bwd_len):
    group_rows, neighbours = fwd_idx.shape
    fwd = fwd_idx.T
    copies = jnp.broadcast_to(sources.T[None], (Z * X,) + sources.T.shape)
    gathered = exchange(copies, TGT, GATHER)
    tgt_float = targets.astype(jnp.float32)
    tgt_scale = lax.rsqrt(jnp.sum(tgt_float * tgt_float, axis=1) + 1e-06).reshape(-1, LANES)
    sent = call(
        score_kernel, (24, LANES),
        gathered, targets, tgt_scale, bwd_idx.T, bwd_len.reshape(-1, LANES), fwd,
    )
    other = lax.ppermute(sent[:8], "core", [(0, 1), (1, 0)])
    sent = call(join_kernel, (X * Y, 24, LANES), sent, other)
    got = exchange(sent, ("x", "y"), SUM)
    sent = call(mean_kernel, (Z, 32, LANES), got, fwd)
    got = exchange(sent, "z", SPREAD)
    return call(margin_kernel, (neighbours, group_rows), got).T


def solution(mesh):
    grid = Mesh(mesh.devices.reshape(Z, X, Y, CORE), TGT + SRC)
    in_specs = (P(SRC, TGT), P(TGT, None), P(SRC, None), P(TGT, None), P(TGT))
    return jax.shard_map(body, mesh=grid, in_specs=in_specs, out_specs=P(SRC, None), check_vma=False)
```

```python
import jax
import jax.numpy as jnp
from jax import lax
from jax.experimental import pallas as pl
from jax.experimental.pallas import tpu as pltpu
from jax.sharding import Mesh, PartitionSpec as P

Z, X, Y, CORE = 8, 4, 4, 2
TGT = ("z", "x")
SRC = ("y", "core")
GATHER = [((z + 4) % Z) * X + (x + 2) % X for x in (0, 3, 2, 1) for z in range(Z)]
SUM = [((x + 2) % X) * Y + (y + 2) % Y for x in range(X) for y in range(Y)]
SPREAD = [(z + 4) % Z for z in (0, 4, 3, 5, 2, 6, 1, 7)]
LANES = 128
VMEM_BYTES = 24 * 1024 * 1024


def take_rows(rows, index):
    return jnp.take_along_axis(rows, index, axis=0)


def take_lanes(rows, index):
    return jnp.take_along_axis(rows, index, axis=1)


def pick_from_tiles(block, index, first_row, picked):
    tile, row = index >> 3, index & 7
    for i in range(block.shape[0] // 8):
        match = tile == (first_row // 8 + i)
        rows = block[8 * i : 8 * i + 8, :]
        picked = [
            jnp.where(match[8 * h : 8 * h + 8], take_rows(rows, row[8 * h : 8 * h + 8]), picked[h])
            for h in range(len(picked))
        ]
    return picked


def pick_from_table(table, index):
    high, low = index >> 7, index & 127
    picked = [jnp.zeros((8, LANES), jnp.float32)] * 2
    for i in range(table.shape[0]):
        row = jnp.broadcast_to(table[i : i + 1, :], (8, LANES))
        picked = [
            jnp.where(high[8 * h : 8 * h + 8] == i, take_lanes(row, low[8 * h : 8 * h + 8]), picked[h])
            for h in range(2)
        ]
    return jnp.concatenate(picked, axis=0)


def score_kernel(src_ref, tgt_ref, scale_ref, bwd_ref, len_ref, fwd_ref, out_ref):
    src = jnp.concatenate([src_ref[GATHER.index(t)] for t in range(Z * X)], axis=0)
    src_float = src.astype(jnp.float32)
    src_scale = lax.rsqrt(jnp.sum(src_float * src_float, axis=0, keepdims=True) + 1e-06)
    fwd_local = fwd_ref[...] - lax.axis_index(TGT) * tgt_ref.shape[0]
    first_src = lax.axis_index(SRC) * LANES
    neighbour = lax.broadcasted_iota(jnp.int32, (16, LANES), 0)
    cos = [jnp.zeros((8, LANES), jnp.float32)] * 2
    tgt_scale, back = scale_ref[...], []
    for c in range(tgt_ref.shape[0] // LANES):
        lanes = slice(LANES * c, LANES * c + LANES)
        block = jnp.dot(tgt_ref[lanes, :], src, preferred_element_type=jnp.float32) * src_scale
        cos = pick_from_tiles(block, fwd_local, LANES * c, cos)
        zero = [jnp.zeros((8, LANES), jnp.float32)] * 2
        sims = jnp.concatenate(pick_from_tiles(block.T, bwd_ref[:, lanes] - first_src, 0, zero), axis=0)
        length = len_ref[c : c + 1, :]
        total = jnp.sum(jnp.where(neighbour < length, sims, 0.0), axis=0, keepdims=True)
        back.append(total * tgt_scale[c : c + 1, :] / length.astype(jnp.float32))
    cos = jnp.concatenate(cos, axis=0) * pick_from_table(tgt_scale, fwd_local)
    out_ref[...] = jnp.concatenate(back + [cos], axis=0)


def join_kernel(own_ref, other_ref, out_ref):
    total = own_ref[:8, :] + other_ref[...]
    for d in range(out_ref.shape[0]):
        out_ref[d, :8, :] = total
        out_ref[d, 8:, :] = own_ref[8:, :]


def mean_kernel(got_ref, fwd_ref, out_ref):
    y = lax.axis_index("y")
    first_tgt = lax.axis_index("z") * (X * 8 * LANES)
    table, cos = [], jnp.zeros((16, LANES), jnp.float32)
    for x in range(X):
        parts = [SUM.index(x * Y + line) for line in range(Y)]
        total = got_ref[parts[0], :8, :]
        for at in parts[1:]:
            total = total + got_ref[at, :8, :]
        table.append(total)
        for line, at in enumerate(parts):
            cos = cos + jnp.where(y == line, got_ref[at, 8:, :], 0.0)
    bwd = pick_from_table(jnp.concatenate(table, axis=0), fwd_ref[...] - first_tgt)
    for d in range(out_ref.shape[0]):
        out_ref[d, :16, :] = cos
        out_ref[d, 16:, :] = bwd


def margin_kernel(got_ref, out_ref):
    total = jnp.sum(got_ref[...], axis=0)
    cos, bwd = total[:16], total[16:]
    fwd_mean = jnp.mean(cos, axis=0, keepdims=True)
    out_ref[...] = cos / ((fwd_mean + bwd) * 0.5)


def call(kernel, shape, *args):
    return pl.pallas_call(
        kernel,
        out_shape=jax.ShapeDtypeStruct(shape, jnp.float32),
        in_specs=[pl.BlockSpec(memory_space=pltpu.VMEM)] * len(args),
        out_specs=pl.BlockSpec(memory_space=pltpu.VMEM),
        compiler_params=pltpu.CompilerParams(vmem_limit_bytes=VMEM_BYTES),
    )(*args)


def exchange(blocks, axes, order):
    return lax.all_to_all(blocks, axes, 0, 0, axis_index_groups=[order])


def body(sources, targets, fwd_idx, bwd_idx, bwd_len):
    group_rows, neighbours = fwd_idx.shape
    fwd = fwd_idx.T
    copies = jnp.broadcast_to(sources.T[None], (Z * X,) + sources.T.shape)
    gathered = exchange(copies, TGT, GATHER)
    tgt_float = targets.astype(jnp.float32)
    tgt_scale = lax.rsqrt(jnp.sum(tgt_float * tgt_float, axis=1) + 1e-06).reshape(-1, LANES)
    sent = call(
        score_kernel, (24, LANES),
        gathered, targets, tgt_scale, bwd_idx.T, bwd_len.reshape(-1, LANES), fwd,
    )
    other = lax.ppermute(sent[:8], "core", [(0, 1), (1, 0)])
    sent = call(join_kernel, (X * Y, 24, LANES), sent, other)
    got = exchange(sent, ("x", "y"), SUM)
    sent = call(mean_kernel, (Z, 32, LANES), got, fwd)
    got = exchange(sent, "z", SPREAD)
    return call(margin_kernel, (neighbours, group_rows), got).T


def solution(mesh):
    grid = Mesh(mesh.devices.reshape(Z, X, Y, CORE), TGT + SRC)
    in_specs = (P(SRC, TGT), P(TGT, None), P(SRC, None), P(TGT, None), P(TGT))
    return jax.shard_map(body, mesh=grid, in_specs=in_specs, out_specs=P(SRC, None), check_vma=False)
```

```python
import jax
import jax.numpy as jnp
from jax import lax
from jax.experimental import pallas as pl
from jax.experimental.pallas import tpu as pltpu
from jax.sharding import Mesh, PartitionSpec as P

Z, X, Y, CORE = 8, 4, 4, 2
TGT = ("z", "x")
SRC = ("y", "core")
GATHER = [((z + 4) % Z) * X + (x + 2) % X for x in (0, 3, 2, 1) for z in range(Z)]
SUM = [((x + 2) % X) * Y + (y + 2) % Y for x in (0, 3, 2, 1) for y in range(Y)]
SPREAD = [(z + 4) % Z for z in (0, 4, 3, 5, 2, 6, 1, 7)]
LANES = 128
VMEM_BYTES = 24 * 1024 * 1024


def take_rows(rows, index):
    return jnp.take_along_axis(rows, index, axis=0)


def take_lanes(rows, index):
    return jnp.take_along_axis(rows, index, axis=1)


def pick_from_tiles(block, index, first_row, picked):
    tile, row = index >> 3, index & 7
    for i in range(block.shape[0] // 8):
        match = tile == (first_row // 8 + i)
        rows = block[8 * i : 8 * i + 8, :]
        picked = [
            jnp.where(match[8 * h : 8 * h + 8], take_rows(rows, row[8 * h : 8 * h + 8]), picked[h])
            for h in range(len(picked))
        ]
    return picked


def pick_from_table(table, index):
    high, low = index >> 7, index & 127
    picked = [jnp.zeros((8, LANES), jnp.float32)] * 2
    for i in range(table.shape[0]):
        row = jnp.broadcast_to(table[i : i + 1, :], (8, LANES))
        picked = [
            jnp.where(high[8 * h : 8 * h + 8] == i, take_lanes(row, low[8 * h : 8 * h + 8]), picked[h])
            for h in range(2)
        ]
    return jnp.concatenate(picked, axis=0)


def score_kernel(src_ref, tgt_ref, scale_ref, bwd_ref, len_ref, out_ref, block_ref):
    src = jnp.concatenate([src_ref[GATHER.index(t)] for t in range(Z * X)], axis=0)
    src_float = src.astype(jnp.float32)
    src_scale = lax.rsqrt(jnp.sum(src_float * src_float, axis=0, keepdims=True) + 1e-06)
    first_src = lax.axis_index(SRC) * LANES
    neighbour = lax.broadcasted_iota(jnp.int32, (16, LANES), 0)
    tgt_scale, back = scale_ref[...], []
    for c in range(tgt_ref.shape[0] // LANES):
        lanes = slice(LANES * c, LANES * c + LANES)
        block = jnp.dot(tgt_ref[lanes, :], src, preferred_element_type=jnp.float32) * src_scale
        block_ref[lanes, :] = block
        zero = [jnp.zeros((8, LANES), jnp.float32)] * 2
        sims = jnp.concatenate(pick_from_tiles(block.T, bwd_ref[:, lanes] - first_src, 0, zero), axis=0)
        length = len_ref[c : c + 1, :]
        total = jnp.sum(jnp.where(neighbour < length, sims, 0.0), axis=0, keepdims=True)
        back.append(total * tgt_scale[c : c + 1, :] / length.astype(jnp.float32))
    out_ref[...] = jnp.concatenate(back, axis=0)


def forward_kernel(block_ref, scale_ref, fwd_ref, out_ref):
    fwd_local = fwd_ref[...] - lax.axis_index(TGT) * block_ref.shape[0]
    cos = [jnp.zeros((8, LANES), jnp.float32)] * 2
    cos = jnp.concatenate(pick_from_tiles(block_ref[...], fwd_local, 0, cos), axis=0)
    out_ref[...] = cos * pick_from_table(scale_ref[...], fwd_local)


def join_kernel(own_ref, other_ref, cos_ref, out_ref):
    total = own_ref[...] + other_ref[...]
    for d in range(out_ref.shape[0]):
        out_ref[d, :8, :] = total
        out_ref[d, 8:, :] = cos_ref[...]


def mean_kernel(got_ref, fwd_ref, out_ref):
    y = lax.axis_index("y")
    first_tgt = lax.axis_index("z") * (X * 8 * LANES)
    table, cos = [], jnp.zeros((16, LANES), jnp.float32)
    for x in range(X):
        parts = [SUM.index(x * Y + line) for line in range(Y)]
        total = got_ref[parts[0], :8, :]
        for at in parts[1:]:
            total = total + got_ref[at, :8, :]
        table.append(total)
        for line, at in enumerate(parts):
            cos = cos + jnp.where(y == line, got_ref[at, 8:, :], 0.0)
    bwd = pick_from_table(jnp.concatenate(table, axis=0), fwd_ref[...] - first_tgt)
    for d in range(out_ref.shape[0]):
        out_ref[d, :16, :] = cos
        out_ref[d, 16:, :] = bwd


def margin_kernel(got_ref, out_ref):
    total = jnp.sum(got_ref[...], axis=0)
    cos, bwd = total[:16], total[16:]
    fwd_mean = jnp.mean(cos, axis=0, keepdims=True)
    out_ref[...] = cos / ((fwd_mean + bwd) * 0.5)


def call(kernel, shapes, *args):
    return pl.pallas_call(
        kernel,
        out_shape=[jax.ShapeDtypeStruct(shape, jnp.float32) for shape in shapes],
        in_specs=[pl.BlockSpec(memory_space=pltpu.VMEM)] * len(args),
        out_specs=[pl.BlockSpec(memory_space=pltpu.VMEM)] * len(shapes),
        compiler_params=pltpu.CompilerParams(vmem_limit_bytes=VMEM_BYTES),
    )(*args)


def exchange(blocks, axes, order):
    return lax.all_to_all(blocks, axes, 0, 0, axis_index_groups=[order])


def body(sources, targets, fwd_idx, bwd_idx, bwd_len):
    group_rows, neighbours = fwd_idx.shape
    fwd = fwd_idx.T
    copies = jnp.broadcast_to(sources.T[None], (Z * X,) + sources.T.shape)
    gathered = exchange(copies, TGT, GATHER)
    tgt_float = targets.astype(jnp.float32)
    tgt_scale = lax.rsqrt(jnp.sum(tgt_float * tgt_float, axis=1) + 1e-06).reshape(-1, LANES)
    back, scores = call(
        score_kernel, [(8, LANES), (targets.shape[0], group_rows)],
        gathered, targets, tgt_scale, bwd_idx.T, bwd_len.reshape(-1, LANES),
    )
    other = lax.ppermute(back, "core", [(0, 1), (1, 0)])
    (cos,) = call(forward_kernel, [(neighbours, group_rows)], scores, tgt_scale, fwd)
    (sent,) = call(join_kernel, [(X * Y, 24, LANES)], back, other, cos)
    got = exchange(sent, ("x", "y"), SUM)
    (sent,) = call(mean_kernel, [(Z, 32, LANES)], got, fwd)
    got = exchange(sent, "z", SPREAD)
    return call(margin_kernel, [(neighbours, group_rows)], got)[0].T


def solution(mesh):
    grid = Mesh(mesh.devices.reshape(Z, X, Y, CORE), TGT + SRC)
    in_specs = (P(SRC, TGT), P(TGT, None), P(SRC, None), P(TGT, None), P(TGT))
    return jax.shard_map(body, mesh=grid, in_specs=in_specs, out_specs=P(SRC, None), check_vma=False)
```

```python
import jax
import jax.numpy as jnp
from jax import lax
from jax.experimental import pallas as pl
from jax.experimental.pallas import tpu as pltpu
from jax.sharding import Mesh, PartitionSpec as P

Z, X, Y, CORE = 8, 4, 4, 2
TGT = ("z", "x")
SRC = ("y", "core")
GATHER = [((z + 4) % Z) * X + (x + 2) % X for x in (0, 3, 2, 1) for z in range(Z)]
SUM = [((x + 2) % X) * Y + (y + 2) % Y for x in (0, 3, 2, 1) for y in range(Y)]
SPREAD = [(z + 4) % Z for z in (0, 4, 3, 5, 2, 6, 1, 7)]
LANES = 128
VMEM_BYTES = 24 * 1024 * 1024


def take_rows(rows, index):
    return jnp.take_along_axis(rows, index, axis=0)


def take_lanes(rows, index):
    return jnp.take_along_axis(rows, index, axis=1)


def pick_from_tiles(block, index, first_row, picked):
    tile, row = index >> 3, index & 7
    for i in range(block.shape[0] // 8):
        match = tile == (first_row // 8 + i)
        rows = block[8 * i : 8 * i + 8, :]
        picked = [
            jnp.where(match[8 * h : 8 * h + 8], take_rows(rows, row[8 * h : 8 * h + 8]), picked[h])
            for h in range(len(picked))
        ]
    return picked


def pick_from_table(table, index):
    high, low = index >> 7, index & 127
    picked = [jnp.zeros((8, LANES), jnp.float32)] * 2
    for i in range(table.shape[0]):
        row = jnp.broadcast_to(table[i : i + 1, :], (8, LANES))
        picked = [
            jnp.where(high[8 * h : 8 * h + 8] == i, take_lanes(row, low[8 * h : 8 * h + 8]), picked[h])
            for h in range(2)
        ]
    return jnp.concatenate(picked, axis=0)


def copy_kernel(src_ref, out_ref):
    block = src_ref[...]
    for d in range(out_ref.shape[0]):
        out_ref[d] = block


def score_kernel(src_ref, tgt_ref, scale_ref, bwd_ref, len_ref, fwd_ref, out_ref):
    src = jnp.concatenate([src_ref[GATHER.index(t)] for t in range(Z * X)], axis=0)
    src_float = src.astype(jnp.float32)
    src_scale = lax.rsqrt(jnp.sum(src_float * src_float, axis=0, keepdims=True) + 1e-06)
    fwd_local = fwd_ref[...] - lax.axis_index(TGT) * tgt_ref.shape[0]
    first_src = lax.axis_index(SRC) * LANES
    neighbour = lax.broadcasted_iota(jnp.int32, (16, LANES), 0)
    cos = [jnp.zeros((8, LANES), jnp.float32)] * 2
    tgt_scale, back = scale_ref[...], []
    for c in range(tgt_ref.shape[0] // LANES):
        lanes = slice(LANES * c, LANES * c + LANES)
        block = jnp.dot(tgt_ref[lanes, :], src, preferred_element_type=jnp.float32) * src_scale
        cos = pick_from_tiles(block, fwd_local, LANES * c, cos)
        zero = [jnp.zeros((8, LANES), jnp.float32)] * 2
        sims = jnp.concatenate(pick_from_tiles(block.T, bwd_ref[:, lanes] - first_src, 0, zero), axis=0)
        length = len_ref[c : c + 1, :]
        total = jnp.sum(jnp.where(neighbour < length, sims, 0.0), axis=0, keepdims=True)
        back.append(total * tgt_scale[c : c + 1, :] / length.astype(jnp.float32))
    cos = jnp.concatenate(cos, axis=0) * pick_from_table(tgt_scale, fwd_local)
    out_ref[...] = jnp.concatenate(back + [cos], axis=0)


def join_kernel(own_ref, other_ref, out_ref):
    total = own_ref[:8, :] + other_ref[...]
    for d in range(out_ref.shape[0]):
        out_ref[d, :8, :] = total
        out_ref[d, 8:, :] = own_ref[8:, :]


def mean_kernel(got_ref, fwd_ref, out_ref):
    y = lax.axis_index("y")
    first_tgt = lax.axis_index("z") * (X * 8 * LANES)
    table, cos = [], jnp.zeros((16, LANES), jnp.float32)
    for x in range(X):
        parts = [SUM.index(x * Y + line) for line in range(Y)]
        total = got_ref[parts[0], :8, :]
        for at in parts[1:]:
            total = total + got_ref[at, :8, :]
        table.append(total)
        for line, at in enumerate(parts):
            cos = cos + jnp.where(y == line, got_ref[at, 8:, :], 0.0)
    bwd = pick_from_table(jnp.concatenate(table, axis=0), fwd_ref[...] - first_tgt)
    for d in range(out_ref.shape[0]):
        out_ref[d, :16, :] = cos
        out_ref[d, 16:, :] = bwd


def margin_kernel(got_ref, out_ref):
    total = jnp.sum(got_ref[...], axis=0)
    cos, bwd = total[:16], total[16:]
    fwd_mean = jnp.mean(cos, axis=0, keepdims=True)
    out_ref[...] = cos / ((fwd_mean + bwd) * 0.5)


def call(kernel, shape, *args, dtype=jnp.float32):
    return pl.pallas_call(
        kernel,
        out_shape=jax.ShapeDtypeStruct(shape, dtype),
        in_specs=[pl.BlockSpec(memory_space=pltpu.VMEM)] * len(args),
        out_specs=pl.BlockSpec(memory_space=pltpu.VMEM),
        compiler_params=pltpu.CompilerParams(vmem_limit_bytes=VMEM_BYTES),
    )(*args)


def exchange(blocks, axes, order):
    return lax.all_to_all(blocks, axes, 0, 0, axis_index_groups=[order])


def body(sources, targets, fwd_idx, bwd_idx, bwd_len):
    group_rows, neighbours = fwd_idx.shape
    fwd = fwd_idx.T
    copies = call(copy_kernel, (Z * X,) + sources.T.shape, sources.T, dtype=sources.dtype)
    gathered = exchange(copies, TGT, GATHER)
    tgt_float = targets.astype(jnp.float32)
    tgt_scale = lax.rsqrt(jnp.sum(tgt_float * tgt_float, axis=1) + 1e-06).reshape(-1, LANES)
    sent = call(
        score_kernel, (24, LANES),
        gathered, targets, tgt_scale, bwd_idx.T, bwd_len.reshape(-1, LANES), fwd,
    )
    other = lax.ppermute(sent[:8], "core", [(0, 1), (1, 0)])
    sent = call(join_kernel, (X * Y, 24, LANES), sent, other)
    got = exchange(sent, ("x", "y"), SUM)
    sent = call(mean_kernel, (Z, 32, LANES), got, fwd)
    got = exchange(sent, "z", SPREAD)
    return call(margin_kernel, (neighbours, group_rows), got).T


def solution(mesh):
    grid = Mesh(mesh.devices.reshape(Z, X, Y, CORE), TGT + SRC)
    in_specs = (P(SRC, TGT), P(TGT, None), P(SRC, None), P(TGT, None), P(TGT))
    return jax.shard_map(body, mesh=grid, in_specs=in_specs, out_specs=P(SRC, None), check_vma=False)
```

```python
import jax
import jax.numpy as jnp
from jax import lax
from jax.experimental import pallas as pl
from jax.experimental.pallas import tpu as pltpu
from jax.sharding import Mesh, PartitionSpec as P

Z, X, Y, CORE = 8, 4, 4, 2
TGT = ("z", "x")
SRC = ("y", "core")
GATHER = [((z + 4) % Z) * X + (x + 2) % X for x in (0, 3, 2, 1) for z in range(Z)]
SUM = [((x + 2) % X) * Y + (y + 2) % Y for x in (0, 3, 2, 1) for y in range(Y)]
SPREAD = [(z + 4) % Z for z in (0, 4, 3, 5, 2, 6, 1, 7)]
LANES = 128
VMEM_BYTES = 24 * 1024 * 1024


def take_rows(rows, index):
    return jnp.take_along_axis(rows, index, axis=0)


def take_lanes(rows, index):
    return jnp.take_along_axis(rows, index, axis=1)


def pick_from_tiles(block, index, first_row, picked):
    tile, row = index >> 3, index & 7
    for i in range(block.shape[0] // 8):
        match = tile == (first_row // 8 + i)
        rows = block[8 * i : 8 * i + 8, :]
        picked = [
            jnp.where(match[8 * h : 8 * h + 8], take_rows(rows, row[8 * h : 8 * h + 8]), picked[h])
            for h in range(len(picked))
        ]
    return picked


def pick_from_table(table, index):
    high, low = index >> 7, index & 127
    picked = [jnp.zeros((8, LANES), jnp.float32)] * 2
    for i in range(table.shape[0]):
        row = jnp.broadcast_to(table[i : i + 1, :], (8, LANES))
        picked = [
            jnp.where(high[8 * h : 8 * h + 8] == i, take_lanes(row, low[8 * h : 8 * h + 8]), picked[h])
            for h in range(2)
        ]
    return jnp.concatenate(picked, axis=0)


def score_kernel(src_ref, tgt_ref, scale_ref, bwd_ref, len_ref, fwd_ref, out_ref):
    src = jnp.concatenate([src_ref[GATHER.index(t)] for t in range(Z * X)], axis=0)
    src_float = src.astype(jnp.float32)
    src_scale = lax.rsqrt(jnp.sum(src_float * src_float, axis=0, keepdims=True) + 1e-06)
    fwd_local = fwd_ref[...] - lax.axis_index(TGT) * tgt_ref.shape[0]
    first_src = lax.axis_index(SRC) * LANES
    neighbour = lax.broadcasted_iota(jnp.int32, (16, LANES), 0)
    cos = [jnp.zeros((8, LANES), jnp.float32)] * 2
    tgt_scale, back = scale_ref[...], []
    for c in range(tgt_ref.shape[0] // LANES):
        lanes = slice(LANES * c, LANES * c + LANES)
        block = jnp.dot(tgt_ref[lanes, :], src, preferred_element_type=jnp.float32) * src_scale
        cos = pick_from_tiles(block, fwd_local, LANES * c, cos)
        zero = [jnp.zeros((8, LANES), jnp.float32)] * 2
        sims = jnp.concatenate(pick_from_tiles(block.T, bwd_ref[:, lanes] - first_src, 0, zero), axis=0)
        length = len_ref[c : c + 1, :]
        total = jnp.sum(jnp.where(neighbour < length, sims, 0.0), axis=0, keepdims=True)
        back.append(total * tgt_scale[c : c + 1, :] / length.astype(jnp.float32))
    cos = jnp.concatenate(cos, axis=0) * pick_from_table(tgt_scale, fwd_local)
    out_ref[...] = jnp.concatenate(back + [cos], axis=0)


def join_kernel(own_ref, other_ref, out_ref):
    total = own_ref[:8, :] + other_ref[...]
    for d in range(out_ref.shape[0]):
        out_ref[d, :8, :] = total
        out_ref[d, 8:, :] = own_ref[8:, :]


def mean_kernel(got_ref, fwd_ref, out_ref):
    y = lax.axis_index("y")
    first_tgt = lax.axis_index("z") * (X * 8 * LANES)
    table, cos = [], jnp.zeros((16, LANES), jnp.float32)
    for x in range(X):
        parts = [SUM.index(x * Y + line) for line in range(Y)]
        total = got_ref[parts[0], :8, :]
        for at in parts[1:]:
            total = total + got_ref[at, :8, :]
        table.append(total)
        for line, at in enumerate(parts):
            cos = cos + jnp.where(y == line, got_ref[at, 8:, :], 0.0)
    bwd = pick_from_table(jnp.concatenate(table, axis=0), fwd_ref[...] - first_tgt)
    for d in range(out_ref.shape[0]):
        out_ref[d, :16, :] = cos
        out_ref[d, 16:, :] = bwd


def margin_kernel(got_ref, out_ref):
    total = jnp.sum(got_ref[...], axis=0)
    cos, bwd = total[:16], total[16:]
    fwd_mean = jnp.mean(cos, axis=0, keepdims=True)
    out_ref[...] = cos / ((fwd_mean + bwd) * 0.5)


def call(kernel, shape, *args):
    return pl.pallas_call(
        kernel,
        out_shape=jax.ShapeDtypeStruct(shape, jnp.float32),
        in_specs=[pl.BlockSpec(memory_space=pltpu.VMEM)] * len(args),
        out_specs=pl.BlockSpec(memory_space=pltpu.VMEM),
        compiler_params=pltpu.CompilerParams(vmem_limit_bytes=VMEM_BYTES),
    )(*args)


def exchange(blocks, axes, order):
    return lax.all_to_all(blocks, axes, 0, 0, axis_index_groups=[order])


def body(sources, targets, fwd_idx, bwd_idx, bwd_len):
    group_rows, neighbours = fwd_idx.shape
    fwd = fwd_idx.T
    copies = jnp.broadcast_to(sources.T[None], (Z * X,) + sources.T.shape)
    gathered = exchange(copies, TGT, GATHER)
    tgt_float = targets.astype(jnp.float32)
    tgt_scale = lax.rsqrt(jnp.sum(tgt_float * tgt_float, axis=1) + 1e-06).reshape(-1, LANES)
    sent = call(
        score_kernel, (24, LANES),
        gathered, targets, tgt_scale, bwd_idx.T, bwd_len.reshape(-1, LANES), fwd,
    )
    other = lax.ppermute(sent[:8], "core", [(0, 1), (1, 0)])
    sent = call(join_kernel, (X * Y, 24, LANES), sent, other)
    got = exchange(sent, ("x", "y"), SUM)
    sent = call(mean_kernel, (Z, 32, LANES), got, fwd)
    got = exchange(sent, "z", SPREAD)
    return call(margin_kernel, (neighbours, group_rows), got).T


def solution(mesh):
    grid = Mesh(mesh.devices.reshape(Z, X, Y, CORE), TGT + SRC)
    in_specs = (P(SRC, TGT), P(TGT, None), P(SRC, None), P(TGT, None), P(TGT))
    return jax.shard_map(body, mesh=grid, in_specs=in_specs, out_specs=P(SRC, None), check_vma=False)
```
